256 devices in a mesh: hst: 32 (over z, y), local: 8 (over x, core).
Axes of the slice: x: 4, y: 4, z: 8, core: 2. Of those that a mesh axis runs over, the one named last changes fastest.
Arguments:
- embedding: float32 [524288, 256], P(('hst', 'local')), may hold values from -6 to 6
- row_accum: float32 [524288], P(('hst', 'local')), may hold values from 0.5 to 8
- lookup_grads: bfloat16 [524288, 256], P(('hst', 'local')), may hold values from -3 to 3
- lookup_slot: int32 [524288], P(('hst', 'local')), may hold values from 0 to 8191, as said below
- owner_rows: int32 [256, 32, 32], P(('hst', 'local')), may hold values from -1 to 2047, as said below
Outputs:
- new_embedding: float32 [524288, 256], P(('hst', 'local'))
- new_accum: float32 [524288], P(('hst', 'local'))
- fresh_rows: bfloat16 [524288, 256], P(('hst', 'local'))
The draws below stay inside these ranges and needn't reach their ends.
Inputs may be any that keep to these rules, and one draw needn't show every extreme that they name: For a lookup of host s, lookup_slot = o * 32 + c with owner device o and c below that host's count of live slots for o; owners with low numbers are looked up far more often. owner_rows[o, s, c] is live (not -1) exactly for c below a count of 1 to 32; every (o, s) with o mod 32 equal to s has 32 live slots; live rows of one (o, s) are distinct; a few leading slots name the same row for every host s.
All inputs are finite; a program needn't handle non-finite values.
Results may differ from the reference program's by a relative error of at most 0.0039.
Values may be sent and summed in bfloat16 or wider, within the bound.
A program may use at most 64 MiB of HBM per device.

```python
import math
import jax
import jax.numpy as jnp
from jax import lax

E = 256
ROWS_DEV = 2048
TOK_DEV = 2048
CAP = 32
OWNERS = 256
TOKENS = 524288
TABLE_ROWS = 524288
N_HST = 32
N_LOCAL = 8


def bucket_counts(key):
    key = jax.random.fold_in(key, 100)
    counts = jax.random.randint(key, (N_HST, OWNERS), 1, CAP + 1)
    is_full = jnp.arange(OWNERS)[None, :] % N_HST == jnp.arange(N_HST)[:, None]
    return jnp.where(is_full, CAP, counts).astype(jnp.int32)


def draw_lookup_slot(key, part):
    counts = bucket_counts(key)
    key = jax.random.fold_in(key, 1)
    key_a, key_b, key_c, key_d = jax.random.split(key, 4)
    pick_a = jax.random.randint(key_a, (TOKENS,), 0, OWNERS)
    pick_b = jax.random.randint(key_b, (TOKENS,), 0, OWNERS)
    pick_c = jax.random.randint(key_c, (TOKENS,), 0, OWNERS)
    owner_pick = jnp.minimum(pick_a, jnp.minimum(pick_b, pick_c))
    host_of = jnp.arange(TOKENS) // (TOK_DEV * N_LOCAL)
    host_count = counts[host_of, owner_pick]
    position = jax.random.randint(key_d, (TOKENS,), 0, CAP) % host_count
    slots = owner_pick * CAP + position
    token_pos = jnp.arange(TOKENS)
    slots = jnp.where(token_pos == TOKENS - 1, OWNERS * CAP - 1, slots)
    slots = jnp.where(token_pos == 0, 0, slots)
    return slots.astype(jnp.int32)


def draw_owner_rows(key, part):
    counts = bucket_counts(key)
    key = jax.random.fold_in(key, 2)
    key_a, key_b = jax.random.split(key, 2)
    span_rows = ROWS_DEV // CAP
    base_pick = jax.random.randint(key_a, (OWNERS, N_HST, CAP), 0, span_rows)
    shared = jax.random.randint(key_b, (OWNERS, 1, CAP), 0, span_rows)
    slot_pos = jnp.arange(CAP)[None, None, :]
    is_hot = slot_pos < max(1, CAP // 4)
    corner = (jnp.arange(OWNERS)[:, None, None] == 0) & (jnp.arange(N_HST)[None, :, None] == 0) & (slot_pos == CAP - 1)
    base_pick = jnp.where(corner, span_rows - 1, base_pick)
    local_row = slot_pos * span_rows + jnp.where(is_hot, shared, base_pick)
    is_live = slot_pos < counts.T[:, :, None]
    return jnp.where(is_live, local_row, -1).astype(jnp.int32)


def levels(key, extent, cuts, smallest, largest):
    def one(dim, parts):
        steps = jax.random.uniform(jax.random.fold_in(jax.random.fold_in(key, 6), dim), (parts,), jnp.float32, smallest / len(cuts), largest / len(cuts))
        return jnp.repeat(jnp.exp(steps), extent[dim] // parts).reshape((-1,) + (1,) * (len(extent) - dim - 1))

    loudness = one(*cuts[0])
    for cut in cuts[1:]:
        loudness = loudness * one(*cut)
    return loudness


def normal_values(stream_key, shape, width, limit, cuts=(), kind=jnp.bfloat16):
    level = levels(stream_key, shape, cuts, -0.22, 0.18) if cuts else 1.0
    result = jax.random.normal(stream_key, shape, jnp.float32) * width * level
    return jnp.minimum(jnp.maximum(result, -limit), limit).astype(kind)


def setup_inputs(seed: int = 0) -> dict:
    keys = jax.random.split(jax.random.key(seed), 6)
    return {
        "embedding": normal_values(keys[0], (TABLE_ROWS, E), 1.0, 6.0, ((0, 256),), jnp.float32),
        "row_accum": jnp.clip(jnp.exp(math.log(8.0) - 2.7725887 * jax.random.uniform(keys[1], (TABLE_ROWS,), jnp.float32) ** levels(keys[1], (TABLE_ROWS,), ((0, 256),), -0.2, 0.2)), 0.5, 8.0),
        "lookup_grads": normal_values(keys[2], (TOKENS, E), 0.5, 3.0, ((0, 256),)),
        "lookup_slot": draw_lookup_slot(jax.random.fold_in(keys[5], 71), 0),
        "owner_rows": draw_owner_rows(jax.random.fold_in(keys[5], 71), 0),
    }


def reference(embedding, row_accum, lookup_grads, lookup_slot, owner_rows):
    n_owner = N_HST * N_LOCAL
    slot_total = n_owner * CAP
    grad_blocks = lookup_grads.reshape(n_owner, TOK_DEV, E)
    slot_blocks = lookup_slot.reshape(n_owner, TOK_DEV)

    def add_device(carry, device):
        grad_part = lax.dynamic_index_in_dim(grad_blocks, device, 0, keepdims=False)
        slot_part = lax.dynamic_index_in_dim(slot_blocks, device, 0, keepdims=False)
        partial_value = jax.ops.segment_sum(grad_part.astype(jnp.float32), slot_part, num_segments=slot_total)
        partial_value = lax.optimization_barrier(partial_value.astype(jnp.bfloat16)).astype(jnp.float32)
        host_of = device // N_LOCAL
        return (carry.at[host_of].add(partial_value), None)
    start = jnp.zeros((N_HST, slot_total, E), jnp.float32)
    slot_grad, _ = lax.scan(add_device, start, jnp.arange(n_owner, dtype=jnp.int32))
    slot_grad = lax.optimization_barrier(slot_grad.astype(jnp.bfloat16)).astype(jnp.float32)
    grid = slot_grad.reshape(N_HST, n_owner, CAP, E).transpose(1, 0, 2, 3).reshape(-1, E)
    owner_base = (jnp.arange(n_owner, dtype=jnp.int32) * ROWS_DEV)[:, None, None]
    is_live = owner_rows >= 0
    target = jnp.where(is_live, owner_rows + owner_base, TABLE_ROWS).astype(jnp.int32)
    row_grad = jax.ops.segment_sum(grid, target.reshape(-1), num_segments=TABLE_ROWS + 1)[:TABLE_ROWS]
    new_accum = row_accum + lax.optimization_barrier(jnp.mean(row_grad * row_grad, axis=1))
    new_embedding = embedding - 0.1 * row_grad / jnp.sqrt(new_accum)[:, None]
    safe_rows = jnp.where(is_live, target, 0).astype(jnp.int32)
    picked = jnp.take(new_embedding, safe_rows.reshape(-1), axis=0).reshape(n_owner, N_HST, CAP, E)
    picked = jnp.where(is_live[:, :, :, None], picked, 0.0).astype(jnp.bfloat16)
    host_cache = picked.transpose(1, 0, 2, 3).reshape(N_HST * slot_total, E)
    host_of = jnp.arange(TOKENS, dtype=jnp.int32) // (TOK_DEV * N_LOCAL)
    fresh_rows = jnp.take(host_cache, host_of * slot_total + lookup_slot, axis=0)
    return (new_embedding, new_accum, fresh_rows)
```

```python
import functools

import jax
import jax.numpy as jnp
from jax import lax
from jax.experimental import pallas as pl
from jax.experimental.pallas import tpu as pltpu
from jax.sharding import PartitionSpec as P

MESH = pl.DeviceIdType.MESH
F32 = jnp.float32
BF16 = jnp.bfloat16
NY = 4
LANES = 128


def plane_dz(plane, nz):
    group, half = divmod(plane, 2)
    if half == 0:
        return nz // 2 - group
    return (nz // 2 + group) % nz if group else 0


def plane_of(dz, nz):
    return next(p for p in range(nz) if plane_dz(p, nz) == dz % nz)


def kernel(
    nz, ny, cap,
    slot_ref, g_hbm, orow_ref, accum_ref, emb_hbm,
    newemb_hbm, newacc_ref, fresh_ref,
    slots, g_all, fkey, facc, fsend, frecv, fin, grecv, rg, emb_v, embbf, pick, cache, ekey, gacc,
    load_sem, d2d_send, d2d_recv, fs_sem, fr_sem, as_sem, ar_sem, rs_sem, rr_sem, gs_sem, gr_sem, out_sem,
):
    n_hst = nz * ny
    tokens, feat = g_hbm.shape
    rows = emb_hbm.shape[0]
    nt = tokens // LANES
    n_groups = nz // 2
    plane_rows = ny * cap

    h = lax.axis_index("hst")
    l = lax.axis_index("local")
    z, y = h // ny, h % ny
    x, core = l // 2, l % 2
    right = lax.rem(x + 1, 4) * 2 + core
    left = lax.rem(x + 3, 4) * 2 + core
    sib = x * 2 + 1 - core

    barrier = pltpu.get_barrier_semaphore()

    def greet(d, carry):
        peer = lax.rem(h + d, n_hst)
        pl.semaphore_signal(barrier, inc=1, device_id=(peer, l), device_id_type=MESH)
        return carry

    for peer in (sib, right, left):
        pl.semaphore_signal(barrier, inc=1, device_id=(h, peer), device_id_type=MESH)
    lax.fori_loop(1, n_hst, greet, 0)

    load_g = pltpu.make_async_copy(g_hbm, g_all.at[0], load_sem.at[0])
    load_g.start()
    load_e = pltpu.make_async_copy(emb_hbm, emb_v, load_sem.at[1])
    load_e.start()

    def remote(src, dst, ssem, rsem, hh, ll):
        return pltpu.make_async_remote_copy(
            src_ref=src, dst_ref=dst, send_sem=ssem, recv_sem=rsem, device_id=(hh, ll), device_id_type=MESH
        )

    def decode(s):
        position = s % cap
        owner = s // cap
        ol = owner % 8
        oh = owner // 8
        lo = (oh % ny) * cap + position
        dz = (oh // ny - z + nz) % nz
        half = jnp.where((dz >= 1) & (dz <= nz // 2), 0, 1)
        group = jnp.where(half == 0, nz // 2 - dz, jnp.where(dz == 0, 0, dz - nz // 2))
        dx = (ol // 2 - x + 4) % 4
        dcore = (ol % 2 - core + 2) % 2
        return lo, group, half, dx, dcore

    def forward_key(s):
        lo, group, half, dx, dcore = decode(s)
        return jnp.where(dcore == 0, (group * 8 + dx * 2 + half) * LANES + lo, -4096).astype(F32)

    own_slots = slot_ref[...]
    fkey[0] = forward_key(own_slots)

    pl.semaphore_wait(barrier, n_hst - 1 + 3)

    d2d = [
        remote(slot_ref, slots, d2d_send.at[0], d2d_recv.at[0], h, sib),
        remote(g_hbm, g_all.at[1], d2d_send.at[1], d2d_recv.at[1], h, sib),
    ]
    for c in d2d:
        c.start()

    sub_iota = lax.broadcasted_iota(jnp.int32, (LANES, LANES), 0)
    lane_iota = lax.broadcasted_iota(jnp.int32, (LANES, LANES), 1)
    sub_bf = sub_iota.astype(F32).astype(BF16)
    one = jnp.ones((LANES, LANES), BF16)
    zero = jnp.zeros((LANES, LANES), BF16)

    def row_hot(key_row, base):
        rel = jnp.broadcast_to(key_row - base, (LANES, LANES)).astype(BF16)
        return jnp.where(rel == sub_bf, one, zero)

    kt = min(512, tokens)
    per_tile = kt // LANES

    def forward_part(group, core_index):
        def step(k, carry):
            hot = []
            for b in range(8):
                base = float((group * 8 + b) * LANES)
                hot.append(
                    jnp.concatenate(
                        [row_hot(fkey[core_index, pl.ds(k * per_tile + i, 1), :], base) for i in range(per_tile)], axis=1
                    )
                )
            hot = jnp.concatenate(hot, axis=0)
            part = jnp.dot(
                hot, g_all[core_index, pl.ds(pl.multiple_of(k * kt, kt), kt), :], preferred_element_type=F32
            )
            facc[group] += part.reshape(8, plane_rows, feat)
            return carry

        lax.fori_loop(0, tokens // kt, step, 0)

    block_of = (4, 5, 3, 6, 2, 7)

    def forward_send(group, index, value):
        fsend[group, index] = value.astype(BF16)
        c = remote(
            fsend.at[group, index], frecv.at[group, index], fs_sem.at[group, index], fr_sem.at[group, index],
            h, right if index in (0, 2, 4) else left,
        )
        c.start()
        return c

    sends = []

    def fwait(group, index):
        remote(
            fsend.at[group, index], frecv.at[group, index], fs_sem.at[group, index], fr_sem.at[group, index], h, right
        ).wait_recv()

    def merge(group):
        for index, far in ((4, 0), (5, 1)):
            fwait(group, far)
            sends.append(
                forward_send(group, index, facc[group, block_of[index]] + frecv[group, far].astype(F32))
            )

    def scatter_hosts(src_plane, dst_plane, ssem, rsem, dz):
        for dy in range(ny):
            if dz == 0 and dy == 0:
                continue
            py = lax.rem(y + dy, ny)
            peer = lax.rem(z + dz, nz) * ny + py
            remote(src_plane.at[py], dst_plane.at[y], ssem, rsem, peer, l).start()

    def wait_hosts(src_plane, dst_plane, ssem, rsem, dz, what):
        count = ny - 1 if dz == 0 else ny
        c = remote(src_plane.at[pl.ds(0, count)], dst_plane.at[pl.ds(0, count)], ssem, rsem, h, sib)
        c.wait_send() if what == "send" else c.wait_recv()

    def finalize(group):
        for half, (from_left, from_right) in enumerate(((4, 3), (2, 5))):
            plane = 2 * group + half
            dz = plane_dz(plane, nz)
            back = plane_of(-dz, nz)
            fwait(group, from_left)
            fwait(group, from_right)
            total = facc[group, half] + frecv[group, from_left].astype(F32) + frecv[group, from_right].astype(F32)
            fin[plane] = total.astype(BF16).reshape(ny, cap, feat)
            scatter_hosts(fin.at[plane], grecv.at[back], as_sem.at[plane], ar_sem.at[back], dz)
            if dz == 0:
                grecv[plane, y] = fin[plane, y]

    rg[...] = jnp.zeros_like(rg)

    def owner_row(plane):
        return orow_ref[pl.ds(lax.rem(z + plane_dz(plane, nz), nz), 1), :].astype(F32)

    def accumulate(group):
        planes = (2 * group, 2 * group + 1)
        for plane in planes:
            wait_hosts(fin.at[plane], grecv.at[plane], as_sem.at[plane], ar_sem.at[plane], plane_dz(plane, nz), "recv")
        data = grecv[pl.ds(2 * group, 2)].reshape(2 * plane_rows, feat)
        keys = [owner_row(plane) for plane in planes]
        span = min(512, rows)

        def step(r, carry):
            start = pl.multiple_of(r * span, span)
            base = (r * span).astype(F32)
            hot = jnp.concatenate(
                [
                    jnp.concatenate([row_hot(key, base + float(i * LANES)) for key in keys], axis=1)
                    for i in range(span // LANES)
                ],
                axis=0,
            )
            rg[pl.ds(start, span), :] += jnp.dot(hot, data, preferred_element_type=F32)
            return carry

        lax.fori_loop(0, rows // span, step, 0)

    load_g.wait()
    for group in range(n_groups):
        facc[group] = jnp.zeros((8, plane_rows, feat), F32)
        forward_part(group, 0)
        if group == 0:
            for c in d2d:
                c.wait()
            fkey[1] = forward_key(slots[...])
        forward_part(group, 1)
        for index in (0, 1, 2, 3):
            sends.append(forward_send(group, index, facc[group, block_of[index]]))
        if group >= 1:
            merge(group - 1)
        if group >= 2:
            finalize(group - 2)
    if n_groups >= 2:
        finalize(n_groups - 2)
    merge(n_groups - 1)

    def column(row):
        return jnp.broadcast_to(row.astype(F32), (LANES, LANES)).T.astype(jnp.int32)

    def column_key(hi, lo):
        return jnp.where(lane_iota == column(lo), column(hi), -1).astype(F32).astype(BF16)

    lo, group_, half_, dx, dcore = decode(own_slots)
    hi = (dx * 2 + dcore) * nz + group_ * 2 + half_
    for i in range(nt):
        ekey[pl.ds(i * LANES, LANES), :] = column_key(hi[i : i + 1, :], lo[i : i + 1, :])
    load_e.wait()
    gacc[...] = jnp.zeros_like(gacc)

    for group in range(max(n_groups - 2, 0)):
        accumulate(group)
    finalize(n_groups - 1)
    for group in range(max(n_groups - 2, 0), n_groups):
        accumulate(group)

    eye = sub_iota == lane_iota

    def update(i, carry):
        start = pl.multiple_of(i * LANES, LANES)
        grad = rg[pl.ds(start, LANES), :]
        mean = jnp.sum(grad * grad, axis=1, keepdims=True) * (1.0 / feat)
        old = jnp.broadcast_to(accum_ref[pl.ds(i, 1), :], (LANES, LANES)).T
        new = old + mean
        newacc_ref[pl.ds(i, 1), :] = jnp.sum(jnp.where(eye, new, 0.0), axis=0, keepdims=True)
        scale = 0.1 / jnp.sqrt(new)
        scale = jnp.concatenate([scale] * (feat // LANES), axis=1)
        fresh = emb_v[pl.ds(start, LANES), :] - grad * scale
        emb_v[pl.ds(start, LANES), :] = fresh
        embbf[pl.ds(start, LANES), :] = fresh.astype(BF16)
        return carry

    lax.fori_loop(0, rows // LANES, update, 0)
    store_e = pltpu.make_async_copy(emb_v, newemb_hbm, out_sem.at[0])
    store_e.start()

    one_c = jnp.ones((2 * plane_rows, LANES), BF16)
    zero_c = jnp.zeros((2 * plane_rows, LANES), BF16)

    def send_back(group):
        key = jnp.concatenate(
            [
                column_key(jnp.floor(owner_row(p) * (1.0 / LANES)), owner_row(p) - LANES * jnp.floor(owner_row(p) * (1.0 / LANES)))
                for p in (2 * group, 2 * group + 1)
            ],
            axis=0,
        )
        hot = jnp.concatenate(
            [jnp.where(key == jnp.asarray(b, BF16), one_c, zero_c) for b in range(rows // LANES)], axis=1
        )
        got = jnp.dot(hot, embbf[...], preferred_element_type=F32).astype(BF16)
        for half in range(2):
            plane = 2 * group + half
            dz = plane_dz(plane, nz)
            back = plane_of(-dz, nz)
            pick[plane] = got[half * plane_rows : (half + 1) * plane_rows].reshape(ny, cap, feat)
            scatter_hosts(pick.at[plane], cache.at[0, back], rs_sem.at[plane], rr_sem.at[back], dz)
            if dz == 0:
                cache[0, plane, y] = pick[plane, y]

    def gather_copy(group, index):
        pair, first, second = pl.ds(2 * group, 2), 2 * group, 2 * group + 1
        src, dst, to = (
            (cache.at[0, pair], cache.at[6, pair], right),
            (cache.at[0, pair], cache.at[2, pair], left),
            (cache.at[0, pair], cache.at[1, pair], sib),
            (cache.at[6, pair], cache.at[7, pair], sib),
            (cache.at[6, first], cache.at[4, first], right),
            (cache.at[2, pair], cache.at[3, pair], sib),
            (cache.at[2, second], cache.at[4, second], left),
            (cache.at[4, first], cache.at[5, first], sib),
            (cache.at[4, second], cache.at[5, second], sib),
        )[index]
        return remote(src, dst, gs_sem.at[group, index], gr_sem.at[group, index], h, to)

    def own_arrived(group):
        for plane in (2 * group, 2 * group + 1):
            wait_hosts(
                pick.at[plane], cache.at[0, plane], rs_sem.at[plane], rr_sem.at[plane], plane_dz(plane, nz), "recv"
            )
        for index in (0, 1, 2):
            gather_copy(group, index).start()

    def near_arrived(group):
        gather_copy(group, 0).wait_recv()
        gather_copy(group, 4).start()
        gather_copy(group, 3).start()
        gather_copy(group, 1).wait_recv()
        gather_copy(group, 6).start()
        gather_copy(group, 5).start()

    def far_arrived(group):
        gather_copy(group, 4).wait_recv()
        gather_copy(group, 7).start()
        gather_copy(group, 6).wait_recv()
        gather_copy(group, 8).start()

    tt = min(512, tokens)
    one_g = jnp.ones((tt, LANES), BF16)
    zero_g = jnp.zeros((tt, LANES), BF16)

    def look_up(chunks, last=False):
        for lane, group in chunks:
            for index in {1: (2,), 7: (3,), 3: (5,), 5: (7, 8)}.get(lane, ()):
                gather_copy(group, index).wait_recv()

        def step(i, carry):
            span = pl.ds(pl.multiple_of(i * tt, tt), tt)
            key = ekey[span, :]
            total = gacc[span, :]
            for lane, group in chunks:
                first = lane * nz + 2 * group
                hot = jnp.concatenate(
                    [jnp.where(key == jnp.asarray(b, BF16), one_g, zero_g) for b in (first, first + 1)], axis=1
                )
                data = cache[lane, pl.ds(2 * group, 2)].reshape(2 * plane_rows, feat)
                total += jnp.dot(hot, data, preferred_element_type=F32)
            if last:
                fresh_ref[span, :] = total.astype(BF16)
            else:
                gacc[span, :] = total
            return carry

        lax.fori_loop(0, tokens // tt, step, 0)

    order = list(range(n_groups - 1, -1, -1))
    for group in order:
        send_back(group)
    for i, group in enumerate(order):
        own_arrived(group)
        if i >= 1:
            near_arrived(order[i - 1])
            look_up([(0, group), (1, order[i - 1])])
        else:
            look_up([(0, group)])
        if i >= 2:
            far_arrived(order[i - 2])
            look_up([(6, order[i - 2]), (2, order[i - 2]), (7, order[i - 2]), (3, order[i - 2])])
        if i >= 3:
            look_up([(4, order[i - 3]), (5, order[i - 3])])
    near_arrived(order[-1])
    look_up([(1, order[-1])])
    if n_groups >= 2:
        far_arrived(order[-2])
        look_up([(6, order[-2]), (2, order[-2]), (7, order[-2]), (3, order[-2])])
    if n_groups >= 3:
        look_up([(4, order[-3]), (5, order[-3])])
    look_up([(6, order[-1]), (2, order[-1]), (7, order[-1]), (3, order[-1])])
    far_arrived(order[-1])
    if n_groups >= 2:
        look_up([(4, order[-2]), (5, order[-2])])
    look_up([(4, order[-1]), (5, order[-1])], last=True)

    store_e.wait()
    for c in sends:
        c.wait_send()
    for plane in range(nz):
        dz = plane_dz(plane, nz)
        wait_hosts(fin.at[plane], grecv.at[plane], as_sem.at[plane], ar_sem.at[plane], dz, "send")
        wait_hosts(pick.at[plane], cache.at[0, plane], rs_sem.at[plane], rr_sem.at[plane], dz, "send")
    for group in range(n_groups):
        for index in range(9):
            gather_copy(group, index).wait_send()


def local(ny, embedding, row_accum, lookup_grads, lookup_slot, owner_rows):
    n_hst = lax.axis_size("hst")
    nz = n_hst // ny
    rows, feat = embedding.shape
    tokens = lookup_slot.shape[0]
    cap = owner_rows.shape[2]
    nt = tokens // LANES
    groups = nz // 2
    plane = ny * cap
    vmem = pl.BlockSpec(memory_space=pltpu.VMEM)
    hbm = pl.BlockSpec(memory_space=pl.ANY)
    dma = pltpu.SemaphoreType.DMA
    new_embedding, new_accum, fresh = pl.pallas_call(
        functools.partial(kernel, nz, ny, cap),
        out_shape=(
            jax.ShapeDtypeStruct((rows, feat), F32),
            jax.ShapeDtypeStruct((rows // LANES, LANES), F32),
            jax.ShapeDtypeStruct((tokens, feat), BF16),
        ),
        in_specs=[vmem, hbm, vmem, vmem, hbm],
        out_specs=(hbm, vmem, vmem),
        scratch_shapes=[
            pltpu.VMEM((nt, LANES), jnp.int32),
            pltpu.VMEM((2, tokens, feat), BF16),
            pltpu.VMEM((2, nt, LANES), F32),
            pltpu.VMEM((groups, 8, plane, feat), F32),
            pltpu.VMEM((groups, 6, plane, feat), BF16),
            pltpu.VMEM((groups, 6, plane, feat), BF16),
            pltpu.VMEM((nz, ny, cap, feat), BF16),
            pltpu.VMEM((nz, ny, cap, feat), BF16),
            pltpu.VMEM((rows, feat), F32),
            pltpu.VMEM((rows, feat), F32),
            pltpu.VMEM((rows, feat), BF16),
            pltpu.VMEM((nz, ny, cap, feat), BF16),
            pltpu.VMEM((8, nz, ny, cap, feat), BF16),
            pltpu.VMEM((tokens, LANES), BF16),
            pltpu.VMEM((tokens, feat), F32),
            dma((2,)),
            dma((2,)),
            dma((2,)),
            dma((groups, 6)),
            dma((groups, 6)),
            dma((nz,)),
            dma((nz,)),
            dma((nz,)),
            dma((nz,)),
            dma((groups, 9)),
            dma((groups, 9)),
            dma((1,)),
        ],
        compiler_params=pltpu.CompilerParams(
            collective_id=0, has_side_effects=True, vmem_limit_bytes=56 * 1024 * 1024
        ),
    )(
        lookup_slot.reshape(nt, LANES),
        lookup_grads,
        owner_rows.reshape(nz, plane),
        row_accum.reshape(rows // LANES, LANES),
        embedding,
    )
    return new_embedding, new_accum.reshape(rows), fresh


def solution(mesh, ny=NY):
    both = ("hst", "local")
    return jax.shard_map(
        functools.partial(local, ny),
        mesh=mesh,
        in_specs=(P(both, None), P(both), P(both, None), P(both), P(both, None, None)),
        out_specs=(P(both, None), P(both), P(both, None)),
        check_vma=False,
    )
```

```python
import functools

import jax
import jax.numpy as jnp
from jax import lax
from jax.experimental import pallas as pl
from jax.experimental.pallas import tpu as pltpu
from jax.sharding import PartitionSpec as P

MESH = pl.DeviceIdType.MESH
F32 = jnp.float32
BF16 = jnp.bfloat16
NY = 4
LANES = 128
SCHEDULES = {
    4: (
        "C0", "c0", "S0", "C1", "c1", "S1", "M0", "C2", "M1", "c2", "S2", "C3", "c3", "Z0", "P", "Z1", "S3", "M2", "M3",
        "Z2", "Z3", "U0", "U1", "o1", "o0", "n1", "n0", "o3", "o2", "L00,01,10,11", "f1", "f0", "L61,21,71,31", "n3",
        "n2", "L60,20,70,30", "f3", "L40,41,50,51", "L02,03,12,13", "f2", "L63,23,73,33", "L62,22,72,32,43,53", "L42,52",
    ),
    2: (
        "C0", "c0", "S0", "M0", "C1", "c1", "S1", "M1", "Z0", "Z1", "P", "U0", "U1", "o0", "n0", "L00,10", "f0",
        "L60,20,70,30", "L40,50", "o1", "n1", "L01,11", "f1", "L61,21,71,31", "L41,51",
    ),
}


def kernel(
    schedule, nz, ny, cap,
    slot_hbm, g_hbm, owner_hbm, accum_hbm, emb_hbm,
    newemb_v, acc_v, fresh_v,
    slots, owner_ref, accum_ref, g_all, fkey, orow, facc, fsend, frecv, fin, grecv, emb_v, embbf, pick, cache, ekey, gacc,
    load_sem, d2d_send, d2d_recv, fs_sem, fr_sem, as_sem, ar_sem, rs_sem, rr_sem, gs_sem, gr_sem,
):
    tokens, feat = g_hbm.shape
    rows = emb_hbm.shape[0]
    nt = tokens // LANES
    n_groups = nz // 2
    n_sub = n_groups // 2
    plane_rows = ny * cap

    h = lax.axis_index("hst")
    l = lax.axis_index("local")
    z, y = h // ny, h % ny
    x, core = l // 2, l % 2
    parity = z % 2
    right = lax.rem(x + 1, 4) * 2 + core
    left = lax.rem(x + 3, 4) * 2 + core
    sib = x * 2 + 1 - core

    barrier = pltpu.get_barrier_semaphore()

    def greet(sem, hh, ll):
        pl.semaphore_signal(sem, inc=1, device_id=(hh, ll), device_id_type=MESH)

    load_s, load_g, load_o, load_a, load_e = [
        pltpu.make_async_copy(src, dst, load_sem.at[i])
        for i, (src, dst) in enumerate(
            (
                (slot_hbm, slots.at[0]),
                (g_hbm, g_all.at[0]),
                (owner_hbm, owner_ref),
                (accum_hbm, accum_ref),
                (emb_hbm, emb_v),
            )
        )
    ]
    for c in (load_s, load_g, load_o, load_a, load_e):
        c.start()

    for peer in (sib, right, left):
        greet(barrier, h, peer)
    for d in range(1, nz * ny):
        greet(barrier, lax.rem(h + d, nz * ny), l)

    def remote(src, dst, ssem, rsem, hh, ll):
        return pltpu.make_async_remote_copy(
            src_ref=src, dst_ref=dst, send_sem=ssem, recv_sem=rsem, device_id=(hh, ll), device_id_type=MESH
        )

    def far_dz(m):
        return nz // 2 - m

    def near_dz(m):
        return jnp.where(m == 0, 0, lax.rem(nz // 2 + m, nz))

    def distance(i):
        return 2 * (i % n_sub) + lax.rem(i // n_sub + parity, 2)

    def plane_z(i, half):
        m = distance(i)
        return lax.rem(z + (near_dz(m) if half else far_dz(m)), nz)

    def decode(s):
        position = s % cap
        owner = s // cap
        ol = owner % 8
        oh = owner // 8
        lo = (oh % ny) * cap + position
        dz = (oh // ny - z + nz) % nz
        half = jnp.where((dz >= 1) & (dz <= nz // 2), 0, 1)
        m = jnp.where(half == 0, nz // 2 - dz, jnp.where(dz == 0, 0, dz - nz // 2))
        group = ((m + parity) % 2) * n_sub + m // 2
        dx = (ol // 2 - x + 4) % 4
        dcore = (ol % 2 - core + 2) % 2
        return lo, group, half, dx, dcore

    def forward_key(s):
        lo, group, half, dx, dcore = decode(s)
        return jnp.where(dcore == 0, (group * 8 + dx * 2 + half) * LANES + lo, -4096).astype(F32)

    load_s.wait()
    own_slots = slots[0]
    fkey[0] = forward_key(own_slots)

    pl.semaphore_wait(barrier, 3 + nz * ny - 1)

    d2d = [
        remote(slot_hbm, slots.at[1], d2d_send.at[0], d2d_recv.at[0], h, sib),
        remote(g_hbm, g_all.at[1], d2d_send.at[1], d2d_recv.at[1], h, sib),
    ]
    for c in d2d:
        c.start()

    sub_iota = lax.broadcasted_iota(jnp.int32, (LANES, LANES), 0)
    lane_iota = lax.broadcasted_iota(jnp.int32, (LANES, LANES), 1)
    sub_bf = sub_iota.astype(F32).astype(BF16)
    one = jnp.ones((LANES, LANES), BF16)
    zero = jnp.zeros((LANES, LANES), BF16)

    def row_hot(key_row, base):
        rel = jnp.broadcast_to(key_row - base, (LANES, LANES)).astype(BF16)
        return jnp.where(rel == sub_bf, one, zero)

    def slot_sums(group, blocks, cores):
        hot = jnp.concatenate(
            [
                jnp.concatenate(
                    [row_hot(fkey[c, i : i + 1, :], float((group * 8 + b) * LANES)) for c in cores for i in range(nt)], axis=1
                )
                for b in blocks
            ],
            axis=0,
        )
        data = g_all[...].reshape(2 * tokens, feat) if len(cores) == 2 else g_all[cores[0]]
        return jnp.dot(hot, data, preferred_element_type=F32).reshape(len(blocks), plane_rows, feat)

    first_blocks, second_blocks = (4, 5, 3, 6), (2, 7, 0, 1)

    def forward_copy(group, index):
        return remote(
            fsend.at[group, index], frecv.at[group, index], fs_sem.at[group, index], fr_sem.at[group, index],
            h, right if index in (0, 2, 4) else left,
        )

    def compute_first(group):
        if group == 0:
            own = slot_sums(group, first_blocks, (0,))
            for c in d2d:
                c.wait()
            fkey[1] = forward_key(slots[1])
            fsend[group, 0:4] = (own + slot_sums(group, first_blocks, (1,))).astype(BF16)
        else:
            fsend[group, 0:4] = slot_sums(group, first_blocks, (0, 1)).astype(BF16)

    def send_first(group):
        for index in range(4):
            forward_copy(group, index).start()

    def compute_second(group):
        facc[group] = slot_sums(group, second_blocks, (0, 1))

    def merge(group):
        for index, far in ((4, 0), (5, 1)):
            forward_copy(group, far).wait_recv()
            fsend[group, index] = (facc[group, far] + frecv[group, far].astype(F32)).astype(BF16)
            forward_copy(group, index).start()

    def finalize(group):
        m = distance(group)
        for half, (from_left, from_right) in enumerate(((4, 3), (2, 5))):
            plane = 2 * group + half
            forward_copy(group, from_left).wait_recv()
            forward_copy(group, from_right).wait_recv()
            total = facc[group, 2 + half] + frecv[group, from_left].astype(F32) + frecv[group, from_right].astype(F32)
            fin[plane] = total.astype(BF16).reshape(ny, cap, feat)
            to_z = plane_z(group, half)
            back = 2 * m + (half if half == 0 else 1)
            back = jnp.where(m == 0, back, 2 * m + 1 - half)
            for dy in range(ny):
                py = lax.rem(y + dy, ny)
                copy = remote(
                    fin.at[plane, py], grecv.at[back, y], as_sem.at[plane], ar_sem.at[back], to_z * ny + py, l
                )
                if half == 1 and dy == 0:
                    mine = pltpu.make_async_copy(fin.at[plane, y], grecv.at[1, y], ar_sem.at[1])
                    pl.when(m == 0)(mine.start)
                    pl.when(m != 0)(copy.start)
                else:
                    copy.start()

    eye = sub_iota == lane_iota
    span = min(512, rows)

    def column(row):
        return jnp.broadcast_to(row.astype(F32), (LANES, LANES)).T.astype(jnp.int32)

    def column_key(hi, lo):
        return jnp.where(lane_iota == column(lo), column(hi), -1).astype(F32).astype(BF16)

    def rel_plane_z(p):
        m, half = divmod(p, 2)
        dz = nz // 2 - m if half == 0 else ((nz // 2 + m) % nz if m else 0)
        return lax.rem(z + dz, nz)

    one_c = jnp.ones((2 * plane_rows, LANES), BF16)
    zero_c = jnp.zeros((2 * plane_rows, LANES), BF16)

    def planes_of(p, count, src, dst, ssem, rsem):
        return remote(src.at[pl.ds(0, count)], dst.at[pl.ds(0, count)], ssem, rsem, h, sib)

    def owner_step():
        for p in range(nz):
            remote(fin.at[p], grecv.at[p], as_sem.at[p], ar_sem.at[p], h, sib).wait_recv()
        data = grecv[...].reshape(nz * plane_rows, feat)
        keys = [orow[pl.ds(rel_plane_z(p), 1), :] for p in range(nz)]

        def update(i, carry):
            base = (i * span).astype(F32)
            hot = jnp.concatenate(
                [
                    jnp.concatenate([row_hot(key, base + float(j * LANES)) for key in keys], axis=1)
                    for j in range(span // LANES)
                ],
                axis=0,
            )
            grads = jnp.dot(hot, data, preferred_element_type=F32)
            for j in range(span // LANES):
                start = pl.multiple_of(i * span + j * LANES, LANES)
                grad = grads[j * LANES : (j + 1) * LANES]
                mean = jnp.sum(grad * grad, axis=1, keepdims=True) * (1.0 / feat)
                at = i * (span // LANES) + j
                old = jnp.broadcast_to(accum_ref[pl.ds(at, 1), :], (LANES, LANES)).T
                new = old + mean
                acc_v[pl.ds(at, 1), :] = jnp.sum(jnp.where(eye, new, 0.0), axis=0, keepdims=True)
                scale = 0.1 / jnp.sqrt(new)
                scale = jnp.concatenate([scale] * (feat // LANES), axis=1)
                fresh = emb_v[pl.ds(start, LANES), :] - grad * scale
                newemb_v[pl.ds(start, LANES), :] = fresh
                embbf[pl.ds(start, LANES), :] = fresh.astype(BF16)
            return carry

        lax.fori_loop(0, rows // span, update, 0)

        for m in range(n_groups - 1, -1, -1):
            key = []
            for p in (2 * m, 2 * m + 1):
                row = orow[pl.ds(rel_plane_z(p), 1), :]
                hi = jnp.floor(row * (1.0 / LANES))
                key.append(column_key(hi, row - LANES * hi))
            key = jnp.concatenate(key, axis=0)
            hot = jnp.concatenate(
                [jnp.where(key == jnp.asarray(b, BF16), one_c, zero_c) for b in range(rows // LANES)], axis=1
            )
            got = jnp.dot(hot, embbf[...], preferred_element_type=F32).astype(BF16)
            for half in range(2):
                p = 2 * m + half
                pick[p] = got[half * plane_rows : (half + 1) * plane_rows].reshape(ny, cap, feat)
                back = 2 * (parity * n_sub + m // 2) + (half if m == 0 else 1 - half)
                to_z = rel_plane_z(p)
                for dy in range(ny):
                    py = lax.rem(y + dy, ny)
                    if p == 1 and dy == 0:
                        pltpu.make_async_copy(pick.at[p, y], cache.at[0, back, y], rr_sem.at[back]).start()
                    else:
                        remote(
                            pick.at[p, py], cache.at[0, back, y], rs_sem.at[p], rr_sem.at[back], to_z * ny + py, l
                        ).start()

    def gather_copy(group, index):
        pair, first, second = pl.ds(2 * group, 2), 2 * group, 2 * group + 1
        src, dst, to = (
            (cache.at[0, pair], cache.at[6, pair], right),
            (cache.at[0, pair], cache.at[2, pair], left),
            (cache.at[0, pair], cache.at[1, pair], sib),
            (cache.at[6, pair], cache.at[7, pair], sib),
            (cache.at[6, first], cache.at[4, first], right),
            (cache.at[2, pair], cache.at[3, pair], sib),
            (cache.at[2, second], cache.at[4, second], left),
            (cache.at[4, first], cache.at[5, first], sib),
            (cache.at[4, second], cache.at[5, second], sib),
        )[index]
        return remote(src, dst, gs_sem.at[group, index], gr_sem.at[group, index], h, to)

    def own_arrived(group):
        for plane in (2 * group, 2 * group + 1):
            remote(pick.at[0], cache.at[0, plane], rs_sem.at[0], rr_sem.at[plane], h, sib).wait_recv()
        for index in (0, 1, 2):
            gather_copy(group, index).start()

    def near_arrived(group):
        for arrived, onward in ((0, (4, 3)), (1, (6, 5))):
            gather_copy(group, arrived).wait_recv()
            for index in onward:
                gather_copy(group, index).start()

    def far_arrived(group):
        for arrived, onward in ((4, 7), (6, 8)):
            gather_copy(group, arrived).wait_recv()
            gather_copy(group, onward).start()

    tt = min(1024, tokens)
    one_g = jnp.ones((tt, LANES), BF16)
    zero_g = jnp.zeros((tt, LANES), BF16)

    def look_up(chunks, first=False, last=False):
        for lane, group in chunks:
            for index in {1: (2,), 7: (3,), 3: (5,), 5: (7, 8)}.get(lane, ()):
                gather_copy(group, index).wait_recv()

        def step(i, carry):
            at = pl.ds(pl.multiple_of(i * tt, tt), tt)
            key = ekey[at, :]
            blocks = [lane * nz + 2 * group + half for lane, group in chunks for half in range(2)]
            hot = jnp.concatenate([jnp.where(key == jnp.asarray(b, BF16), one_g, zero_g) for b in blocks], axis=1)
            data = jnp.concatenate(
                [cache[lane, pl.ds(2 * group, 2)].reshape(2 * plane_rows, feat) for lane, group in chunks], axis=0
            )
            total = jnp.dot(hot, data, preferred_element_type=F32)
            if not first:
                total += gacc[at, :]
            if last:
                fresh_v[at, :] = total.astype(BF16)
            else:
                gacc[at, :] = total
            return carry

        lax.fori_loop(0, tokens // tt, step, 0)

    def prepare():
        load_o.wait()
        lo, group, half, dx, dcore = decode(own_slots)
        hi = (dx * 2 + dcore) * nz + group * 2 + half
        for i in range(nt):
            ekey[pl.ds(i * LANES, LANES), :] = column_key(hi[i : i + 1, :], lo[i : i + 1, :])
        for i in range(nz):
            orow[i : i + 1, :] = jnp.concatenate(
                [owner_ref[i * ny + k : i * ny + k + 1, :] for k in range(ny)], axis=1
            ).astype(F32)

    def owner_class(value):
        @pl.when(parity == value)
        def _():
            owner_step()

    seen, n_looks = [], sum(op[0] == "L" for op in schedule)
    load_g.wait()
    for op in schedule:
        name, args = op[0], [int(c) for c in op[1:] if op[0] != "L"]
        if name == "C":
            compute_first(*args)
        elif name == "c":
            send_first(*args)
        elif name == "S":
            compute_second(*args)
        elif name == "M":
            merge(*args)
        elif name == "Z":
            finalize(*args)
        elif name == "P":
            prepare()
        elif name == "U":
            if args[0] == 0:
                load_a.wait()
                load_e.wait()
            owner_class(*args)
        elif name == "o":
            own_arrived(*args)
        elif name == "n":
            near_arrived(*args)
        elif name == "f":
            far_arrived(*args)
        elif name == "L":
            seen.append(1)
            look_up([(int(t[0]), int(t[1])) for t in op[1:].split(",")], first=len(seen) == 1, last=len(seen) == n_looks)

    for group in range(n_groups):
        for index in range(6):
            forward_copy(group, index).wait_send()
        for index in range(9):
            gather_copy(group, index).wait_send()
    for p in range(nz):
        group, half = divmod(p, 2)
        whole = remote(fin.at[p], grecv.at[p], as_sem.at[p], ar_sem.at[p], h, sib)
        if half == 0 or group % n_sub:
            whole.wait_send()
        else:
            part = remote(
                fin.at[p, pl.ds(0, ny - 1)], grecv.at[p, pl.ds(0, ny - 1)], as_sem.at[p], ar_sem.at[p], h, sib
            )
            m = distance(group)
            pl.when(m == 0)(part.wait_send)
            pl.when(m != 0)(whole.wait_send)
        count = ny - 1 if p == 1 else ny
        remote(
            pick.at[p, pl.ds(0, count)], cache.at[0, p, pl.ds(0, count)], rs_sem.at[p], rr_sem.at[p], h, sib
        ).wait_send()


def hand_over(emb_in, acc_in, fresh_in, emb_out, acc_out, fresh_out, sem):
    copies = []
    for src, dst, pieces in ((emb_in, emb_out, 4), (fresh_in, fresh_out, 2), (acc_in, acc_out, 1)):
        size = src.shape[0] // pieces
        for i in range(pieces):
            part = pl.ds(i * size, size)
            copies.append(pltpu.make_async_copy(src.at[part], dst.at[part], sem.at[len(copies)]))
    for c in copies:
        c.start()
    for c in copies:
        c.wait()


def local(ny, embedding, row_accum, lookup_grads, lookup_slot, owner_rows):
    n_hst = lax.axis_size("hst")
    nz = n_hst // ny
    rows, feat = embedding.shape
    tokens = lookup_slot.shape[0]
    cap = owner_rows.shape[2]
    nt = tokens // LANES
    groups = nz // 2
    plane = ny * cap
    vmem = pl.BlockSpec(memory_space=pltpu.VMEM)
    hbm = pl.BlockSpec(memory_space=pltpu.HBM)
    dma = pltpu.SemaphoreType.DMA
    outs = (
        jax.ShapeDtypeStruct((rows, feat), F32),
        jax.ShapeDtypeStruct((rows // LANES, LANES), F32),
        jax.ShapeDtypeStruct((tokens, feat), BF16),
    )
    results = pl.pallas_call(
        functools.partial(kernel, SCHEDULES[groups], nz, ny, cap),
        out_shape=tuple(pltpu.VMEM(o.shape, o.dtype) for o in outs),
        in_specs=[hbm] * 5,
        out_specs=(vmem, vmem, vmem),
        scratch_shapes=[
            pltpu.VMEM((2, nt, LANES), jnp.int32),
            pltpu.VMEM((n_hst, cap), jnp.int32),
            pltpu.VMEM((rows // LANES, LANES), F32),
            pltpu.VMEM((2, tokens, feat), BF16),
            pltpu.VMEM((2, nt, LANES), F32),
            pltpu.VMEM((nz, LANES), F32),
            pltpu.VMEM((groups, 4, plane, feat), F32),
            pltpu.VMEM((groups, 6, plane, feat), BF16),
            pltpu.VMEM((groups, 6, plane, feat), BF16),
            pltpu.VMEM((nz, ny, cap, feat), BF16),
            pltpu.VMEM((nz, ny, cap, feat), BF16),
            pltpu.VMEM((rows, feat), F32),
            pltpu.VMEM((rows, feat), BF16),
            pltpu.VMEM((nz, ny, cap, feat), BF16),
            pltpu.VMEM((8, nz, ny, cap, feat), BF16),
            pltpu.VMEM((tokens, LANES), BF16),
            pltpu.VMEM((tokens, feat), F32),
            dma((5,)),
            dma((2,)),
            dma((2,)),
            dma((groups, 6)),
            dma((groups, 6)),
            dma((nz,)),
            dma((nz,)),
            dma((nz,)),
            dma((nz,)),
            dma((groups, 9)),
            dma((groups, 9)),
        ],
        compiler_params=pltpu.CompilerParams(
            collective_id=0, has_side_effects=True, vmem_limit_bytes=44 * 1024 * 1024
        ),
    )(
        *(
            pltpu.with_memory_space_constraint(a, pltpu.HBM)
            for a in (
                lookup_slot.reshape(nt, LANES),
                lookup_grads,
                owner_rows.reshape(n_hst, cap),
                row_accum.reshape(rows // LANES, LANES),
                embedding,
            )
        )
    )
    new_embedding, new_accum, fresh = pl.pallas_call(
        hand_over,
        out_shape=outs,
        in_specs=[vmem, vmem, vmem],
        out_specs=(hbm, hbm, hbm),
        scratch_shapes=[dma((7,))],
    )(*(pltpu.with_memory_space_constraint(r, pltpu.VMEM) for r in results))
    return new_embedding, new_accum.reshape(rows), fresh


def solution(mesh, ny=NY):
    both = ("hst", "local")
    return jax.shard_map(
        functools.partial(local, ny),
        mesh=mesh,
        in_specs=(P(both, None), P(both), P(both, None), P(both), P(both, None, None)),
        out_specs=(P(both, None), P(both), P(both, None)),
        check_vma=False,
    )
```

```python
import functools

import jax
import jax.numpy as jnp
from jax import lax
from jax.experimental import pallas as pl
from jax.experimental.pallas import tpu as pltpu
from jax.sharding import PartitionSpec as P

MESH = pl.DeviceIdType.MESH
F32 = jnp.float32
BF16 = jnp.bfloat16
NY = 4
LANES = 128
SCHEDULES = {
    4: (
        "C0", "c0", "S0", "C1", "c1", "S1", "M0", "C2", "M1", "c2", "S2", "C3", "c3", "Z0", "P", "Z1", "S3", "M2", "M3",
        "Z2", "Z3", "U0", "U1", "o1", "o0", "n1", "n0", "o3", "o2", "L00,01,10,11", "f1", "f0", "L61,21,71,31", "n3",
        "n2", "L60,20,70,30", "f3", "L40,41,50,51", "L02,03,12,13", "f2", "L63,23,73,33", "L62,22,72,32,43,53", "L42,52",
    ),
    2: (
        "C0", "c0", "S0", "M0", "C1", "c1", "S1", "M1", "Z0", "Z1", "P", "U0", "U1", "o0", "n0", "L00,10", "f0",
        "L60,20,70,30", "L40,50", "o1", "n1", "L01,11", "f1", "L61,21,71,31", "L41,51",
    ),
}


def kernel(
    schedule, nz, ny, cap,
    slot_hbm, g_hbm, owner_hbm, accum_hbm, emb_hbm,
    newemb_v, acc_v, fresh_v,
    slots, owner_ref, accum_ref, g_all, fkey, orow, facc, fsend, frecv, fin, grecv, emb_v, embbf, pick, cache, ekey, gacc,
    load_sem, d2d_send, d2d_recv, fs_sem, fr_sem, as_sem, ar_sem, rs_sem, rr_sem, gs_sem, gr_sem,
):
    tokens, feat = g_hbm.shape
    rows = emb_hbm.shape[0]
    nt = tokens // LANES
    n_groups = nz // 2
    n_sub = n_groups // 2
    plane_rows = ny * cap

    h = lax.axis_index("hst")
    l = lax.axis_index("local")
    z, y = h // ny, h % ny
    x, core = l // 2, l % 2
    parity = z % 2
    right = lax.rem(x + 1, 4) * 2 + core
    left = lax.rem(x + 3, 4) * 2 + core
    sib = x * 2 + 1 - core

    barrier = pltpu.get_barrier_semaphore()

    def greet(sem, hh, ll):
        pl.semaphore_signal(sem, inc=1, device_id=(hh, ll), device_id_type=MESH)

    load_s, load_g, load_o, load_a, load_e = [
        pltpu.make_async_copy(src, dst, load_sem.at[i])
        for i, (src, dst) in enumerate(
            (
                (slot_hbm, slots.at[0]),
                (g_hbm, g_all.at[0]),
                (owner_hbm, owner_ref),
                (accum_hbm, accum_ref),
                (emb_hbm, emb_v),
            )
        )
    ]
    for c in (load_s, load_g, load_o, load_a, load_e):
        c.start()

    for peer in (sib, right, left):
        greet(barrier, h, peer)
    for d in range(1, nz * ny):
        greet(barrier, lax.rem(h + d, nz * ny), l)

    def remote(src, dst, ssem, rsem, hh, ll):
        return pltpu.make_async_remote_copy(
            src_ref=src, dst_ref=dst, send_sem=ssem, recv_sem=rsem, device_id=(hh, ll), device_id_type=MESH
        )

    def far_dz(m):
        return nz // 2 - m

    def near_dz(m):
        return jnp.where(m == 0, 0, lax.rem(nz // 2 + m, nz))

    def distance(i):
        return 2 * (i % n_sub) + lax.rem(i // n_sub + parity, 2)

    def plane_z(i, half):
        m = distance(i)
        return lax.rem(z + (near_dz(m) if half else far_dz(m)), nz)

    def decode(s):
        position = s % cap
        owner = s // cap
        ol = owner % 8
        oh = owner // 8
        lo = (oh % ny) * cap + position
        dz = (oh // ny - z + nz) % nz
        half = jnp.where((dz >= 1) & (dz <= nz // 2), 0, 1)
        m = jnp.where(half == 0, nz // 2 - dz, jnp.where(dz == 0, 0, dz - nz // 2))
        group = ((m + parity) % 2) * n_sub + m // 2
        dx = (ol // 2 - x + 4) % 4
        dcore = (ol % 2 - core + 2) % 2
        return lo, group, half, dx, dcore

    def forward_key(s):
        lo, group, half, dx, dcore = decode(s)
        return jnp.where(dcore == 0, (group * 8 + dx * 2 + half) * LANES + lo, -4096).astype(F32)

    load_s.wait()
    own_slots = slots[0]
    fkey[0] = forward_key(own_slots)

    pl.semaphore_wait(barrier, 3 + nz * ny - 1)

    d2d = [
        remote(slot_hbm, slots.at[1], d2d_send.at[0], d2d_recv.at[0], h, sib),
        remote(g_hbm, g_all.at[1], d2d_send.at[1], d2d_recv.at[1], h, sib),
    ]
    for c in d2d:
        c.start()

    sub_iota = lax.broadcasted_iota(jnp.int32, (LANES, LANES), 0)
    lane_iota = lax.broadcasted_iota(jnp.int32, (LANES, LANES), 1)
    sub_bf = sub_iota.astype(F32).astype(BF16)
    one = jnp.ones((LANES, LANES), BF16)
    zero = jnp.zeros((LANES, LANES), BF16)

    def row_hot(key_row, base):
        rel = jnp.broadcast_to(key_row - base, (LANES, LANES)).astype(BF16)
        return jnp.where(rel == sub_bf, one, zero)

    def slot_sums(group, blocks, cores):
        hot = jnp.concatenate(
            [
                jnp.concatenate(
                    [row_hot(fkey[c, i : i + 1, :], float((group * 8 + b) * LANES)) for c in cores for i in range(nt)], axis=1
                )
                for b in blocks
            ],
            axis=0,
        )
        data = g_all[...].reshape(2 * tokens, feat) if len(cores) == 2 else g_all[cores[0]]
        return jnp.dot(hot, data, preferred_element_type=F32).reshape(len(blocks), plane_rows, feat)

    first_blocks, second_blocks = (4, 5, 3, 6), (2, 7, 0, 1)

    def forward_copy(group, index):
        return remote(
            fsend.at[group, index], frecv.at[group, index], fs_sem.at[group, index], fr_sem.at[group, index],
            h, right if index in (0, 2, 4) else left,
        )

    def compute_first(group):
        if group == 0:
            own = slot_sums(group, first_blocks, (0,))
            for c in d2d:
                c.wait()
            fkey[1] = forward_key(slots[1])
            fsend[group, 0:4] = (own + slot_sums(group, first_blocks, (1,))).astype(BF16)
        else:
            fsend[group, 0:4] = slot_sums(group, first_blocks, (0, 1)).astype(BF16)

    def send_first(group):
        for index in range(4):
            forward_copy(group, index).start()

    def compute_second(group):
        facc[group] = slot_sums(group, second_blocks, (0, 1))

    def merge(group):
        for index, far in ((4, 0), (5, 1)):
            forward_copy(group, far).wait_recv()
            fsend[group, index] = (facc[group, far] + frecv[group, far].astype(F32)).astype(BF16)
            forward_copy(group, index).start()

    def finalize(group):
        m = distance(group)
        for half, (from_left, from_right) in enumerate(((4, 3), (2, 5))):
            plane = 2 * group + half
            forward_copy(group, from_left).wait_recv()
            forward_copy(group, from_right).wait_recv()
            total = facc[group, 2 + half] + frecv[group, from_left].astype(F32) + frecv[group, from_right].astype(F32)
            fin[plane] = total.astype(BF16).reshape(ny, cap, feat)
            to_z = plane_z(group, half)
            back = 2 * m + (half if half == 0 else 1)
            back = jnp.where(m == 0, back, 2 * m + 1 - half)
            for dy in range(ny):
                py = lax.rem(y + dy, ny)
                copy = remote(
                    fin.at[plane, py], grecv.at[back, y], as_sem.at[plane], ar_sem.at[back], to_z * ny + py, l
                )
                if half == 1 and dy == 0:
                    mine = pltpu.make_async_copy(fin.at[plane, y], grecv.at[1, y], ar_sem.at[1])
                    pl.when(m == 0)(mine.start)
                    pl.when(m != 0)(copy.start)
                else:
                    copy.start()

    eye = sub_iota == lane_iota
    span = min(512, rows)

    def column(row):
        return jnp.broadcast_to(row.astype(F32), (LANES, LANES)).T.astype(jnp.int32)

    def column_key(hi, lo):
        return jnp.where(lane_iota == column(lo), column(hi), -1).astype(F32).astype(BF16)

    def rel_plane_z(p):
        m, half = divmod(p, 2)
        dz = nz // 2 - m if half == 0 else ((nz // 2 + m) % nz if m else 0)
        return lax.rem(z + dz, nz)

    one_c = jnp.ones((2 * plane_rows, LANES), BF16)
    zero_c = jnp.zeros((2 * plane_rows, LANES), BF16)

    def planes_of(p, count, src, dst, ssem, rsem):
        return remote(src.at[pl.ds(0, count)], dst.at[pl.ds(0, count)], ssem, rsem, h, sib)

    def owner_step():
        for p in range(nz):
            remote(fin.at[p], grecv.at[p], as_sem.at[p], ar_sem.at[p], h, sib).wait_recv()
        data = grecv[...].reshape(nz * plane_rows, feat)
        keys = [orow[pl.ds(rel_plane_z(p), 1), :] for p in range(nz)]

        def update(i, carry):
            base = jnp.asarray(i * span, F32)
            hot = jnp.concatenate(
                [
                    jnp.concatenate([row_hot(key, base + float(j * LANES)) for key in keys], axis=1)
                    for j in range(span // LANES)
                ],
                axis=0,
            )
            grads = jnp.dot(hot, data, preferred_element_type=F32)
            for j in range(span // LANES):
                start = pl.multiple_of(i * span + j * LANES, LANES)
                grad = grads[j * LANES : (j + 1) * LANES]
                mean = jnp.sum(grad * grad, axis=1, keepdims=True) * (1.0 / feat)
                at = i * (span // LANES) + j
                old = jnp.broadcast_to(accum_ref[pl.ds(at, 1), :], (LANES, LANES)).T
                new = old + mean
                acc_v[pl.ds(at, 1), :] = jnp.sum(jnp.where(eye, new, 0.0), axis=0, keepdims=True)
                scale = 0.1 / jnp.sqrt(new)
                scale = jnp.concatenate([scale] * (feat // LANES), axis=1)
                fresh = emb_v[pl.ds(start, LANES), :] - grad * scale
                newemb_v[pl.ds(start, LANES), :] = fresh
                embbf[pl.ds(start, LANES), :] = fresh.astype(BF16)
            return carry

        lax.fori_loop(0, rows // span, update, 0, unroll=True)

        for m in range(n_groups - 1, -1, -1):
            key = []
            for p in (2 * m, 2 * m + 1):
                row = orow[pl.ds(rel_plane_z(p), 1), :]
                hi = jnp.floor(row * (1.0 / LANES))
                key.append(column_key(hi, row - LANES * hi))
            key = jnp.concatenate(key, axis=0)
            hot = jnp.concatenate(
                [jnp.where(key == jnp.asarray(b, BF16), one_c, zero_c) for b in range(rows // LANES)], axis=1
            )
            got = jnp.dot(hot, embbf[...], preferred_element_type=F32).astype(BF16)
            for half in range(2):
                p = 2 * m + half
                pick[p] = got[half * plane_rows : (half + 1) * plane_rows].reshape(ny, cap, feat)
                back = 2 * (parity * n_sub + m // 2) + (half if m == 0 else 1 - half)
                to_z = rel_plane_z(p)
                for dy in range(ny):
                    py = lax.rem(y + dy, ny)
                    if p == 1 and dy == 0:
                        pltpu.make_async_copy(pick.at[p, y], cache.at[0, back, y], rr_sem.at[back]).start()
                    else:
                        remote(
                            pick.at[p, py], cache.at[0, back, y], rs_sem.at[p], rr_sem.at[back], to_z * ny + py, l
                        ).start()

    def gather_copy(group, index):
        pair, first, second = pl.ds(2 * group, 2), 2 * group, 2 * group + 1
        src, dst, to = (
            (cache.at[0, first], cache.at[6, first], right),
            (cache.at[0, second], cache.at[2, second], left),
            (cache.at[0, pair], cache.at[1, pair], sib),
            (cache.at[6, pair], cache.at[7, pair], sib),
            (cache.at[6, first], cache.at[4, first], right),
            (cache.at[2, pair], cache.at[3, pair], sib),
            (cache.at[2, second], cache.at[4, second], left),
            (cache.at[4, first], cache.at[5, first], sib),
            (cache.at[4, second], cache.at[5, second], sib),
            (cache.at[0, second], cache.at[6, second], right),
            (cache.at[0, first], cache.at[2, first], left),
        )[index]
        return remote(src, dst, gs_sem.at[group, index], gr_sem.at[group, index], h, to)

    def own_arrived(group):
        for plane in (2 * group, 2 * group + 1):
            remote(pick.at[0], cache.at[0, plane], rs_sem.at[0], rr_sem.at[plane], h, sib).wait_recv()
        for index in (0, 1, 9, 10, 2):
            gather_copy(group, index).start()

    def near_arrived(group):
        for arrived, onward in ((0, 4), (1, 6), (9, 3), (10, 5)):
            gather_copy(group, arrived).wait_recv()
            gather_copy(group, onward).start()

    def far_arrived(group):
        for arrived, onward in ((4, 7), (6, 8)):
            gather_copy(group, arrived).wait_recv()
            gather_copy(group, onward).start()

    tt = min(1024, tokens)
    one_g = jnp.ones((tt, LANES), BF16)
    zero_g = jnp.zeros((tt, LANES), BF16)

    def look_up(chunks, first=False, last=False):
        for lane, group in chunks:
            for index in {1: (2,), 7: (3,), 3: (5,), 5: (7, 8)}.get(lane, ()):
                gather_copy(group, index).wait_recv()

        def step(i, carry):
            at = pl.ds(pl.multiple_of(i * tt, tt), tt)
            key = ekey[at, :]
            blocks = [lane * nz + 2 * group + half for lane, group in chunks for half in range(2)]
            hot = jnp.concatenate([jnp.where(key == jnp.asarray(b, BF16), one_g, zero_g) for b in blocks], axis=1)
            data = jnp.concatenate(
                [cache[lane, pl.ds(2 * group, 2)].reshape(2 * plane_rows, feat) for lane, group in chunks], axis=0
            )
            total = jnp.dot(hot, data, preferred_element_type=F32)
            if not first:
                total += gacc[at, :]
            if last:
                fresh_v[at, :] = total.astype(BF16)
            else:
                gacc[at, :] = total
            return carry

        lax.fori_loop(0, tokens // tt, step, 0, unroll=True)

    def prepare():
        load_o.wait()
        lo, group, half, dx, dcore = decode(own_slots)
        hi = (dx * 2 + dcore) * nz + group * 2 + half
        for i in range(nt):
            ekey[pl.ds(i * LANES, LANES), :] = column_key(hi[i : i + 1, :], lo[i : i + 1, :])
        for i in range(nz):
            orow[i : i + 1, :] = jnp.concatenate(
                [owner_ref[i * ny + k : i * ny + k + 1, :] for k in range(ny)], axis=1
            ).astype(F32)

    def owner_class(value):
        @pl.when(parity == value)
        def _():
            owner_step()

    seen, n_looks = [], sum(op[0] == "L" for op in schedule)
    load_g.wait()
    for op in schedule:
        name, args = op[0], [int(c) for c in op[1:] if op[0] != "L"]
        if name == "C":
            compute_first(*args)
        elif name == "c":
            send_first(*args)
        elif name == "S":
            compute_second(*args)
        elif name == "M":
            merge(*args)
        elif name == "Z":
            finalize(*args)
        elif name == "P":
            prepare()
        elif name == "U":
            if args[0] == 0:
                load_a.wait()
                load_e.wait()
            owner_class(*args)
        elif name == "o":
            own_arrived(*args)
        elif name == "n":
            near_arrived(*args)
        elif name == "f":
            far_arrived(*args)
        elif name == "L":
            seen.append(1)
            look_up([(int(t[0]), int(t[1])) for t in op[1:].split(",")], first=len(seen) == 1, last=len(seen) == n_looks)

    for group in range(n_groups):
        for index in range(6):
            forward_copy(group, index).wait_send()
        for index in range(11):
            gather_copy(group, index).wait_send()
    for p in range(nz):
        group, half = divmod(p, 2)
        whole = remote(fin.at[p], grecv.at[p], as_sem.at[p], ar_sem.at[p], h, sib)
        if half == 0 or group % n_sub:
            whole.wait_send()
        else:
            part = remote(
                fin.at[p, pl.ds(0, ny - 1)], grecv.at[p, pl.ds(0, ny - 1)], as_sem.at[p], ar_sem.at[p], h, sib
            )
            m = distance(group)
            pl.when(m == 0)(part.wait_send)
            pl.when(m != 0)(whole.wait_send)
        count = ny - 1 if p == 1 else ny
        remote(
            pick.at[p, pl.ds(0, count)], cache.at[0, p, pl.ds(0, count)], rs_sem.at[p], rr_sem.at[p], h, sib
        ).wait_send()


def hand_over(emb_in, acc_in, fresh_in, emb_out, acc_out, fresh_out, sem):
    copies = []
    for src, dst, pieces in ((emb_in, emb_out, 4), (fresh_in, fresh_out, 2), (acc_in, acc_out, 1)):
        size = src.shape[0] // pieces
        for i in range(pieces):
            part = pl.ds(i * size, size)
            copies.append(pltpu.make_async_copy(src.at[part], dst.at[part], sem.at[len(copies)]))
    for c in copies:
        c.start()
    for c in copies:
        c.wait()


def local(ny, embedding, row_accum, lookup_grads, lookup_slot, owner_rows):
    n_hst = lax.axis_size("hst")
    nz = n_hst // ny
    rows, feat = embedding.shape
    tokens = lookup_slot.shape[0]
    cap = owner_rows.shape[2]
    nt = tokens // LANES
    groups = nz // 2
    plane = ny * cap
    vmem = pl.BlockSpec(memory_space=pltpu.VMEM)
    hbm = pl.BlockSpec(memory_space=pltpu.HBM)
    dma = pltpu.SemaphoreType.DMA
    outs = (
        jax.ShapeDtypeStruct((rows, feat), F32),
        jax.ShapeDtypeStruct((rows // LANES, LANES), F32),
        jax.ShapeDtypeStruct((tokens, feat), BF16),
    )
    results = pl.pallas_call(
        functools.partial(kernel, SCHEDULES[groups], nz, ny, cap),
        out_shape=tuple(pltpu.VMEM(o.shape, o.dtype) for o in outs),
        in_specs=[hbm] * 5,
        out_specs=(vmem, vmem, vmem),
        scratch_shapes=[
            pltpu.VMEM((2, nt, LANES), jnp.int32),
            pltpu.VMEM((n_hst, cap), jnp.int32),
            pltpu.VMEM((rows // LANES, LANES), F32),
            pltpu.VMEM((2, tokens, feat), BF16),
            pltpu.VMEM((2, nt, LANES), F32),
            pltpu.VMEM((nz, LANES), F32),
            pltpu.VMEM((groups, 4, plane, feat), F32),
            pltpu.VMEM((groups, 6, plane, feat), BF16),
            pltpu.VMEM((groups, 6, plane, feat), BF16),
            pltpu.VMEM((nz, ny, cap, feat), BF16),
            pltpu.VMEM((nz, ny, cap, feat), BF16),
            pltpu.VMEM((rows, feat), F32),
            pltpu.VMEM((rows, feat), BF16),
            pltpu.VMEM((nz, ny, cap, feat), BF16),
            pltpu.VMEM((8, nz, ny, cap, feat), BF16),
            pltpu.VMEM((tokens, LANES), BF16),
            pltpu.VMEM((tokens, feat), F32),
            dma((5,)),
            dma((2,)),
            dma((2,)),
            dma((groups, 6)),
            dma((groups, 6)),
            dma((nz,)),
            dma((nz,)),
            dma((nz,)),
            dma((nz,)),
            dma((groups, 11)),
            dma((groups, 11)),
        ],
        compiler_params=pltpu.CompilerParams(
            collective_id=0, has_side_effects=True, vmem_limit_bytes=44 * 1024 * 1024
        ),
    )(
        *(
            pltpu.with_memory_space_constraint(a, pltpu.HBM)
            for a in (
                lookup_slot.reshape(nt, LANES),
                lookup_grads,
                owner_rows.reshape(n_hst, cap),
                row_accum.reshape(rows // LANES, LANES),
                embedding,
            )
        )
    )
    new_embedding, new_accum, fresh = pl.pallas_call(
        hand_over,
        out_shape=outs,
        in_specs=[vmem, vmem, vmem],
        out_specs=(hbm, hbm, hbm),
        scratch_shapes=[dma((7,))],
    )(*(pltpu.with_memory_space_constraint(r, pltpu.VMEM) for r in results))
    return new_embedding, new_accum.reshape(rows), fresh


def solution(mesh, ny=NY):
    both = ("hst", "local")
    return jax.shard_map(
        functools.partial(local, ny),
        mesh=mesh,
        in_specs=(P(both, None), P(both), P(both, None), P(both), P(both, None, None)),
        out_specs=(P(both, None), P(both), P(both, None)),
        check_vma=False,
    )
```

```python
import functools

import jax
import jax.numpy as jnp
from jax import lax
from jax.experimental import pallas as pl
from jax.experimental.pallas import tpu as pltpu
from jax.sharding import PartitionSpec as P

MESH = pl.DeviceIdType.MESH
F32 = jnp.float32
BF16 = jnp.bfloat16
NY = 4
LANES = 128
SCHEDULES = {
    4: (
        "C0", "c0", "S0", "C1", "c1", "S1", "M0", "C2", "M1", "c2", "S2", "C3", "c3", "Z0", "Z1", "S3", "M2", "M3", "P",
        "Z2", "Z3", "U0", "U1", "o1", "o0", "n1", "n0", "o3", "o2", "L00,01,10,11", "f1", "f0", "L61,21,71,31", "n3",
        "n2", "L60,20,70,30", "f3", "L40,41,50,51", "L02,03,12,13", "f2", "L63,23,73,33", "L62,22,72,32,43,53", "L42,52",
    ),
    2: (
        "C0", "c0", "S0", "M0", "C1", "c1", "S1", "M1", "Z0", "Z1", "P", "U0", "U1", "o0", "n0", "L00,10", "f0",
        "L60,20,70,30", "L40,50", "o1", "n1", "L01,11", "f1", "L61,21,71,31", "L41,51",
    ),
}


def kernel(
    schedule, nz, ny, cap,
    slot_hbm, g_hbm, owner_hbm, accum_hbm, emb_hbm,
    newemb_v, acc_v, fresh_v,
    slots, owner_ref, accum_ref, g_all, fkey, orow, facc, fsend, frecv, fin, grecv, emb_v, embbf, pick, cache, ekey, gacc,
    load_sem, d2d_send, d2d_recv, fs_sem, fr_sem, as_sem, ar_sem, rs_sem, rr_sem, gs_sem, gr_sem,
):
    tokens, feat = g_hbm.shape
    rows = emb_hbm.shape[0]
    nt = tokens // LANES
    n_groups = nz // 2
    n_sub = n_groups // 2
    plane_rows = ny * cap

    h = lax.axis_index("hst")
    l = lax.axis_index("local")
    z, y = h // ny, h % ny
    x, core = l // 2, l % 2
    parity = z % 2
    right = lax.rem(x + 1, 4) * 2 + core
    left = lax.rem(x + 3, 4) * 2 + core
    sib = x * 2 + 1 - core

    barrier = pltpu.get_barrier_semaphore()

    def greet(sem, hh, ll):
        pl.semaphore_signal(sem, inc=1, device_id=(hh, ll), device_id_type=MESH)

    load_s, load_g, load_o, load_a, load_e = [
        pltpu.make_async_copy(src, dst, load_sem.at[i])
        for i, (src, dst) in enumerate(
            (
                (slot_hbm, slots.at[0]),
                (g_hbm, g_all.at[0]),
                (owner_hbm, owner_ref),
                (accum_hbm, accum_ref),
                (emb_hbm, emb_v),
            )
        )
    ]
    for c in (load_s, load_g, load_o, load_a, load_e):
        c.start()

    for peer in (sib, right, left):
        greet(barrier, h, peer)
    for d in range(1, nz * ny):
        greet(barrier, lax.rem(h + d, nz * ny), l)

    def remote(src, dst, ssem, rsem, hh, ll):
        return pltpu.make_async_remote_copy(
            src_ref=src, dst_ref=dst, send_sem=ssem, recv_sem=rsem, device_id=(hh, ll), device_id_type=MESH
        )

    def far_dz(m):
        return nz // 2 - m

    def near_dz(m):
        return jnp.where(m == 0, 0, lax.rem(nz // 2 + m, nz))

    def distance(i):
        return 2 * (i % n_sub) + lax.rem(i // n_sub + parity, 2)

    def plane_z(i, half):
        m = distance(i)
        return lax.rem(z + (near_dz(m) if half else far_dz(m)), nz)

    def decode(s):
        position = s % cap
        owner = s // cap
        ol = owner % 8
        oh = owner // 8
        lo = (oh % ny) * cap + position
        dz = (oh // ny - z + nz) % nz
        half = jnp.where((dz >= 1) & (dz <= nz // 2), 0, 1)
        m = jnp.where(half == 0, nz // 2 - dz, jnp.where(dz == 0, 0, dz - nz // 2))
        group = ((m + parity) % 2) * n_sub + m // 2
        dx = (ol // 2 - x + 4) % 4
        dcore = (ol % 2 - core + 2) % 2
        return lo, group, half, dx, dcore

    def forward_key(s):
        lo, group, half, dx, dcore = decode(s)
        return jnp.where(dcore == 0, (group * 8 + dx * 2 + half) * LANES + lo, -4096).astype(F32)

    load_s.wait()
    own_slots = slots[0]
    fkey[0] = forward_key(own_slots)

    pl.semaphore_wait(barrier, 3 + nz * ny - 1)

    d2d = [
        remote(slot_hbm, slots.at[1], d2d_send.at[0], d2d_recv.at[0], h, sib),
        remote(g_hbm, g_all.at[1], d2d_send.at[1], d2d_recv.at[1], h, sib),
    ]
    for c in d2d:
        c.start()

    sub_iota = lax.broadcasted_iota(jnp.int32, (LANES, LANES), 0)
    lane_iota = lax.broadcasted_iota(jnp.int32, (LANES, LANES), 1)
    sub_bf = sub_iota.astype(F32).astype(BF16)
    one = jnp.ones((LANES, LANES), BF16)
    zero = jnp.zeros((LANES, LANES), BF16)

    def row_hot(key_row, base):
        rel = jnp.broadcast_to(key_row - base, (LANES, LANES)).astype(BF16)
        return jnp.where(rel == sub_bf, one, zero)

    def slot_sums(group, blocks, cores):
        hot = jnp.concatenate(
            [
                jnp.concatenate(
                    [row_hot(fkey[c, i : i + 1, :], float((group * 8 + b) * LANES)) for c in cores for i in range(nt)], axis=1
                )
                for b in blocks
            ],
            axis=0,
        )
        data = g_all[...].reshape(2 * tokens, feat) if len(cores) == 2 else g_all[cores[0]]
        return jnp.dot(hot, data, preferred_element_type=F32).reshape(len(blocks), plane_rows, feat)

    first_blocks, second_blocks = (4, 5, 3, 6), (2, 7, 0, 1)

    def forward_copy(group, index):
        return remote(
            fsend.at[group, index], frecv.at[group, index], fs_sem.at[group, index], fr_sem.at[group, index],
            h, right if index in (0, 2, 4) else left,
        )

    def compute_first(group):
        if group == 0:
            own = slot_sums(group, first_blocks, (0,))
            for c in d2d:
                c.wait()
            fkey[1] = forward_key(slots[1])
            fsend[group, 0:4] = (own + slot_sums(group, first_blocks, (1,))).astype(BF16)
        else:
            fsend[group, 0:4] = slot_sums(group, first_blocks, (0, 1)).astype(BF16)

    def send_first(group):
        for index in range(4):
            forward_copy(group, index).start()

    def compute_second(group):
        facc[group] = slot_sums(group, second_blocks, (0, 1))

    def merge(group):
        for index, far in ((4, 0), (5, 1)):
            forward_copy(group, far).wait_recv()
            fsend[group, index] = (facc[group, far] + frecv[group, far].astype(F32)).astype(BF16)
            forward_copy(group, index).start()

    def finalize(group):
        m = distance(group)
        for half, (from_left, from_right) in enumerate(((4, 3), (2, 5))):
            plane = 2 * group + half
            forward_copy(group, from_left).wait_recv()
            forward_copy(group, from_right).wait_recv()
            total = facc[group, 2 + half] + frecv[group, from_left].astype(F32) + frecv[group, from_right].astype(F32)
            fin[plane] = total.astype(BF16).reshape(ny, cap, feat)
            to_z = plane_z(group, half)
            back = 2 * m + (half if half == 0 else 1)
            back = jnp.where(m == 0, back, 2 * m + 1 - half)
            for dy in range(ny):
                py = lax.rem(y + dy, ny)
                copy = remote(
                    fin.at[plane, py], grecv.at[back, y], as_sem.at[plane], ar_sem.at[back], to_z * ny + py, l
                )
                if half == 1 and dy == 0:
                    mine = pltpu.make_async_copy(fin.at[plane, y], grecv.at[1, y], ar_sem.at[1])
                    pl.when(m == 0)(mine.start)
                    pl.when(m != 0)(copy.start)
                else:
                    copy.start()

    eye = sub_iota == lane_iota
    span = min(512, rows)

    def column(row):
        return jnp.broadcast_to(row.astype(F32), (LANES, LANES)).T.astype(jnp.int32)

    def column_key(hi, lo):
        return jnp.where(lane_iota == column(lo), column(hi), -1).astype(F32).astype(BF16)

    def rel_plane_z(p):
        m, half = divmod(p, 2)
        dz = nz // 2 - m if half == 0 else ((nz // 2 + m) % nz if m else 0)
        return lax.rem(z + dz, nz)

    one_c = jnp.ones((2 * plane_rows, LANES), BF16)
    zero_c = jnp.zeros((2 * plane_rows, LANES), BF16)

    def planes_of(p, count, src, dst, ssem, rsem):
        return remote(src.at[pl.ds(0, count)], dst.at[pl.ds(0, count)], ssem, rsem, h, sib)

    def owner_step():
        keys = [orow[pl.ds(rel_plane_z(p), 1), :] for p in range(nz)]

        def sums(i, planes):
            hot = jnp.concatenate(
                [
                    jnp.concatenate([row_hot(keys[p], float(i * span + j * LANES)) for p in planes], axis=1)
                    for j in range(span // LANES)
                ],
                axis=0,
            )
            data = grecv[planes[0] : planes[-1] + 1].reshape(len(planes) * plane_rows, feat)
            return jnp.dot(hot, data, preferred_element_type=F32)

        def arrived(planes):
            for p in planes:
                remote(fin.at[p], grecv.at[p], as_sem.at[p], ar_sem.at[p], h, sib).wait_recv()

        early, late = range(nz // 2), range(nz // 2, nz)
        arrived(early)
        for i in range(rows // span):
            gacc[pl.ds(i * span, span), :] = sums(i, early)
        arrived(late)

        def update(i):
            grads = gacc[pl.ds(i * span, span), :] + sums(i, late)
            for j in range(span // LANES):
                start = i * span + j * LANES
                grad = grads[j * LANES : (j + 1) * LANES]
                mean = jnp.sum(grad * grad, axis=1, keepdims=True) * (1.0 / feat)
                at = i * (span // LANES) + j
                old = jnp.broadcast_to(accum_ref[pl.ds(at, 1), :], (LANES, LANES)).T
                new = old + mean
                acc_v[pl.ds(at, 1), :] = jnp.sum(jnp.where(eye, new, 0.0), axis=0, keepdims=True)
                scale = 0.1 / jnp.sqrt(new)
                scale = jnp.concatenate([scale] * (feat // LANES), axis=1)
                fresh = emb_v[pl.ds(start, LANES), :] - grad * scale
                newemb_v[pl.ds(start, LANES), :] = fresh
                embbf[pl.ds(start, LANES), :] = fresh.astype(BF16)

        for i in range(rows // span):
            update(i)

        for m in range(n_groups - 1, -1, -1):
            key = []
            for p in (2 * m, 2 * m + 1):
                row = orow[pl.ds(rel_plane_z(p), 1), :]
                hi = jnp.floor(row * (1.0 / LANES))
                key.append(column_key(hi, row - LANES * hi))
            key = jnp.concatenate(key, axis=0)
            hot = jnp.concatenate(
                [jnp.where(key == jnp.asarray(b, BF16), one_c, zero_c) for b in range(rows // LANES)], axis=1
            )
            got = jnp.dot(hot, embbf[...], preferred_element_type=F32).astype(BF16)
            for half in range(2):
                p = 2 * m + half
                pick[p] = got[half * plane_rows : (half + 1) * plane_rows].reshape(ny, cap, feat)
                back = 2 * (parity * n_sub + m // 2) + (half if m == 0 else 1 - half)
                to_z = rel_plane_z(p)
                for dy in range(ny):
                    py = lax.rem(y + dy, ny)
                    if p == 1 and dy == 0:
                        pltpu.make_async_copy(pick.at[p, y], cache.at[0, back, y], rr_sem.at[back]).start()
                    else:
                        remote(
                            pick.at[p, py], cache.at[0, back, y], rs_sem.at[p], rr_sem.at[back], to_z * ny + py, l
                        ).start()

    def gather_copy(group, index):
        pair, first, second = pl.ds(2 * group, 2), 2 * group, 2 * group + 1
        src, dst, to = (
            (cache.at[0, first], cache.at[6, first], right),
            (cache.at[0, second], cache.at[2, second], left),
            (cache.at[0, pair], cache.at[1, pair], sib),
            (cache.at[6, pair], cache.at[7, pair], sib),
            (cache.at[6, first], cache.at[4, first], right),
            (cache.at[2, pair], cache.at[3, pair], sib),
            (cache.at[2, second], cache.at[4, second], left),
            (cache.at[4, first], cache.at[5, first], sib),
            (cache.at[4, second], cache.at[5, second], sib),
            (cache.at[0, second], cache.at[6, second], right),
            (cache.at[0, first], cache.at[2, first], left),
        )[index]
        return remote(src, dst, gs_sem.at[group, index], gr_sem.at[group, index], h, to)

    def own_arrived(group):
        for plane in (2 * group, 2 * group + 1):
            remote(pick.at[0], cache.at[0, plane], rs_sem.at[0], rr_sem.at[plane], h, sib).wait_recv()
        for index in (0, 1, 9, 10, 2):
            gather_copy(group, index).start()

    def near_arrived(group):
        for arrived, onward in ((0, 4), (1, 6), (9, 3), (10, 5)):
            gather_copy(group, arrived).wait_recv()
            gather_copy(group, onward).start()

    def far_arrived(group):
        for arrived, onward in ((4, 7), (6, 8)):
            gather_copy(group, arrived).wait_recv()
            gather_copy(group, onward).start()

    tt = min(1024, tokens)
    one_g = jnp.ones((tt, LANES), BF16)
    zero_g = jnp.zeros((tt, LANES), BF16)

    def look_up(chunks, first=False, last=False):
        for lane, group in chunks:
            for index in {1: (2,), 7: (3,), 3: (5,), 5: (7, 8)}.get(lane, ()):
                gather_copy(group, index).wait_recv()

        def step(i, carry):
            at = pl.ds(pl.multiple_of(i * tt, tt), tt)
            key = ekey[at, :]
            blocks = [lane * nz + 2 * group + half for lane, group in chunks for half in range(2)]
            hot = jnp.concatenate([jnp.where(key == jnp.asarray(b, BF16), one_g, zero_g) for b in blocks], axis=1)
            data = jnp.concatenate(
                [cache[lane, pl.ds(2 * group, 2)].reshape(2 * plane_rows, feat) for lane, group in chunks], axis=0
            )
            total = jnp.dot(hot, data, preferred_element_type=F32)
            if not first:
                total += gacc[at, :]
            if last:
                fresh_v[at, :] = total.astype(BF16)
            else:
                gacc[at, :] = total
            return carry

        lax.fori_loop(0, tokens // tt, step, 0, unroll=True)

    def prepare():
        load_o.wait()
        lo, group, half, dx, dcore = decode(own_slots)
        hi = (dx * 2 + dcore) * nz + group * 2 + half
        for i in range(nt):
            ekey[pl.ds(i * LANES, LANES), :] = column_key(hi[i : i + 1, :], lo[i : i + 1, :])
        for i in range(nz):
            orow[i : i + 1, :] = jnp.concatenate(
                [owner_ref[i * ny + k : i * ny + k + 1, :] for k in range(ny)], axis=1
            ).astype(F32)

    def owner_class(value):
        @pl.when(parity == value)
        def _():
            owner_step()

    seen, n_looks = [], sum(op[0] == "L" for op in schedule)
    load_g.wait()
    for op in schedule:
        name, args = op[0], [int(c) for c in op[1:] if op[0] != "L"]
        if name == "C":
            compute_first(*args)
        elif name == "c":
            send_first(*args)
        elif name == "S":
            compute_second(*args)
        elif name == "M":
            merge(*args)
        elif name == "Z":
            finalize(*args)
        elif name == "P":
            prepare()
        elif name == "U":
            if args[0] == 0:
                load_a.wait()
                load_e.wait()
            owner_class(*args)
        elif name == "o":
            own_arrived(*args)
        elif name == "n":
            near_arrived(*args)
        elif name == "f":
            far_arrived(*args)
        elif name == "L":
            seen.append(1)
            look_up([(int(t[0]), int(t[1])) for t in op[1:].split(",")], first=len(seen) == 1, last=len(seen) == n_looks)

    for group in range(n_groups):
        for index in range(6):
            forward_copy(group, index).wait_send()
        for index in range(11):
            gather_copy(group, index).wait_send()
    for p in range(nz):
        group, half = divmod(p, 2)
        whole = remote(fin.at[p], grecv.at[p], as_sem.at[p], ar_sem.at[p], h, sib)
        if half == 0 or group % n_sub:
            whole.wait_send()
        else:
            part = remote(
                fin.at[p, pl.ds(0, ny - 1)], grecv.at[p, pl.ds(0, ny - 1)], as_sem.at[p], ar_sem.at[p], h, sib
            )
            m = distance(group)
            pl.when(m == 0)(part.wait_send)
            pl.when(m != 0)(whole.wait_send)
        count = ny - 1 if p == 1 else ny
        remote(
            pick.at[p, pl.ds(0, count)], cache.at[0, p, pl.ds(0, count)], rs_sem.at[p], rr_sem.at[p], h, sib
        ).wait_send()


def hand_over(emb_in, acc_in, fresh_in, emb_out, acc_out, fresh_out, sem):
    copies = []
    for src, dst, pieces in ((emb_in, emb_out, 4), (fresh_in, fresh_out, 2), (acc_in, acc_out, 1)):
        size = src.shape[0] // pieces
        for i in range(pieces):
            part = pl.ds(i * size, size)
            copies.append(pltpu.make_async_copy(src.at[part], dst.at[part], sem.at[len(copies)]))
    for c in copies:
        c.start()
    for c in copies:
        c.wait()


def local(ny, embedding, row_accum, lookup_grads, lookup_slot, owner_rows):
    n_hst = lax.axis_size("hst")
    nz = n_hst // ny
    rows, feat = embedding.shape
    tokens = lookup_slot.shape[0]
    cap = owner_rows.shape[2]
    nt = tokens // LANES
    groups = nz // 2
    plane = ny * cap
    vmem = pl.BlockSpec(memory_space=pltpu.VMEM)
    hbm = pl.BlockSpec(memory_space=pltpu.HBM)
    dma = pltpu.SemaphoreType.DMA
    outs = (
        jax.ShapeDtypeStruct((rows, feat), F32),
        jax.ShapeDtypeStruct((rows // LANES, LANES), F32),
        jax.ShapeDtypeStruct((tokens, feat), BF16),
    )
    results = pl.pallas_call(
        functools.partial(kernel, SCHEDULES[groups], nz, ny, cap),
        out_shape=tuple(pltpu.VMEM(o.shape, o.dtype) for o in outs),
        in_specs=[hbm] * 5,
        out_specs=(vmem, vmem, vmem),
        scratch_shapes=[
            pltpu.VMEM((2, nt, LANES), jnp.int32),
            pltpu.VMEM((n_hst, cap), jnp.int32),
            pltpu.VMEM((rows // LANES, LANES), F32),
            pltpu.VMEM((2, tokens, feat), BF16),
            pltpu.VMEM((2, nt, LANES), F32),
            pltpu.VMEM((nz, LANES), F32),
            pltpu.VMEM((groups, 4, plane, feat), F32),
            pltpu.VMEM((groups, 6, plane, feat), BF16),
            pltpu.VMEM((groups, 6, plane, feat), BF16),
            pltpu.VMEM((nz, ny, cap, feat), BF16),
            pltpu.VMEM((nz, ny, cap, feat), BF16),
            pltpu.VMEM((rows, feat), F32),
            pltpu.VMEM((rows, feat), BF16),
            pltpu.VMEM((nz, ny, cap, feat), BF16),
            pltpu.VMEM((8, nz, ny, cap, feat), BF16),
            pltpu.VMEM((tokens, LANES), BF16),
            pltpu.VMEM((tokens, feat), F32),
            dma((5,)),
            dma((2,)),
            dma((2,)),
            dma((groups, 6)),
            dma((groups, 6)),
            dma((nz,)),
            dma((nz,)),
            dma((nz,)),
            dma((nz,)),
            dma((groups, 11)),
            dma((groups, 11)),
        ],
        compiler_params=pltpu.CompilerParams(
            collective_id=0, has_side_effects=True, vmem_limit_bytes=44 * 1024 * 1024
        ),
    )(
        *(
            pltpu.with_memory_space_constraint(a, pltpu.HBM)
            for a in (
                lookup_slot.reshape(nt, LANES),
                lookup_grads,
                owner_rows.reshape(n_hst, cap),
                row_accum.reshape(rows // LANES, LANES),
                embedding,
            )
        )
    )
    new_embedding, new_accum, fresh = pl.pallas_call(
        hand_over,
        out_shape=outs,
        in_specs=[vmem, vmem, vmem],
        out_specs=(hbm, hbm, hbm),
        scratch_shapes=[dma((7,))],
    )(*(pltpu.with_memory_space_constraint(r, pltpu.VMEM) for r in results))
    return new_embedding, new_accum.reshape(rows), fresh


def solution(mesh, ny=NY):
    both = ("hst", "local")
    return jax.shard_map(
        functools.partial(local, ny),
        mesh=mesh,
        in_specs=(P(both, None), P(both), P(both, None), P(both), P(both, None, None)),
        out_specs=(P(both, None), P(both), P(both, None)),
        check_vma=False,
    )
```
